512 devices in a mesh: dp: 64 (over z, y_lo, x), tensor: 8 (over y_hi, core).
Axes of the slice: x: 4, y: 8 (y_hi: 4, y_lo: 2; y = y_hi * 2 + y_lo), z: 8, core: 2. Of those that a mesh axis runs over, the one named last changes fastest.
Arguments:
- current_acts: bfloat16 [49152, 4096], P('dp', 'tensor'), may hold values from -70 to 70
- current_cot: bfloat16 [49152, 1024], P('dp', 'tensor'), may hold values from -56 to 56
- current_ids: int32 [49152], P('dp'), may hold values from 0 to 128004, as said below
- replay_acts: bfloat16 [49152, 4096], P('dp', 'tensor'), may hold values from -92 to 92
- replay_cot: bfloat16 [49152, 1024], P('dp', 'tensor'), may hold values from -70 to 70
- replay_ids: int32 [49152], P('dp'), may hold values from 0 to 128004, as said below
- master_weight: float32 [4096, 1024], P('dp', 'tensor'), may hold values from -0.09375 to 0.09375
- first_moment: float32 [4096, 1024], P('dp', 'tensor'), may hold values from -0.75 to 0.75
- second_moment: float32 [4096, 1024], P('dp', 'tensor'), may hold values from 1e-05 to 0.1
Outputs:
- new_master: float32 [4096, 1024], P('dp', 'tensor')
- new_first: float32 [4096, 1024], P('dp', 'tensor')
- new_second: float32 [4096, 1024], P('dp', 'tensor')
- gathered_weight: bfloat16 [4096, 1024], P(None, 'tensor')
The draws below stay inside these ranges and needn't reach their ends.
Inputs may be any that keep to these rules, and one draw needn't show every extreme that they name: `current_ids`: the first token of every 768 consecutive tokens is never 128004; other ids are below 128004. `replay_ids`: the first token of every 768 consecutive tokens is never 128004; other ids are below 128004.
All inputs are finite; a program needn't handle non-finite values.
Results may differ from the reference program's by a relative error of at most 0.001.
Values may be sent and summed in bfloat16 or wider, within the bound.
A program may use at most 64 MiB of HBM per device.

```python
import math
import jax
import jax.numpy as jnp
from jax import lax

D = 4096
PAD_ID = 128004
TOK_DP = 768
KV = 1024
TOKENS = 49152


def shared_gauss(key, salt, shape):
    return jnp.clip(jax.random.normal(jax.random.fold_in(key, salt), shape, jnp.float32), -4.0, 4.0)


def capped_gauss(key, salt, shape):
    return jnp.clip(jax.random.normal(jax.random.fold_in(key, salt), shape, jnp.float32), -3.0, 3.0)


def feature_scales(key):
    first_key = jax.random.fold_in(key, 31)
    ramp = jnp.exp(jnp.log(10.0) * jnp.arange(D, dtype=jnp.float32) / D)
    rough = jax.random.uniform(first_key, (D,), jnp.float32, 0.7, 1.4)
    return ramp * rough


def head_scales(key):
    first_key = jax.random.fold_in(key, 37)
    return jnp.exp(jnp.log(10.0) * jax.random.uniform(first_key, (KV,), jnp.float32, 0.0, 1.0))


def feature_direction(key):
    return capped_gauss(key, 47, (D,))


def head_direction(key):
    return capped_gauss(key, 53, (KV,))


def token_factors(key, salt):
    batch_key = jax.random.fold_in(key, salt)
    lead_factor = capped_gauss(batch_key, 1, (TOKENS,))
    other_factor = capped_gauss(batch_key, 2, (TOKENS,))
    return (lead_factor, 0.6 * lead_factor + 0.8 * other_factor)


def common_rows(key, salt, strength, direction):
    lead_factor, mixed_factor = token_factors(key, salt)
    return strength * lead_factor[:, None] * direction[None, :]


def common_heads(key, salt, strength, direction):
    lead_factor, mixed_factor = token_factors(key, salt)
    return strength * mixed_factor[:, None] * direction[None, :]


def draw_current_acts(key, part):
    scales = feature_scales(key)
    base_field = shared_gauss(key, 11, (TOKENS, D))
    strength = 0.1
    base_field = base_field + common_rows(key, 41, strength, feature_direction(key))
    return (base_field * scales[None, :]).astype(jnp.bfloat16)


def draw_replay_acts(key, part):
    scales = feature_scales(key)
    base_field = 0.8 * shared_gauss(key, 11, (TOKENS, D)) + 0.6 * shared_gauss(key, 2, (TOKENS, D))
    strength = 0.1
    base_field = base_field + common_rows(key, 43, strength, feature_direction(key))
    return (base_field * scales[None, :]).astype(jnp.bfloat16)


def draw_current_cot(key, part):
    scales = head_scales(key)
    base_field = shared_gauss(key, 23, (TOKENS, KV))
    strength = 0.1
    base_field = base_field + common_heads(key, 41, strength, head_direction(key))
    return (base_field * scales[None, :]).astype(jnp.bfloat16)


def draw_replay_cot(key, part):
    scales = head_scales(key)
    base_field = -0.6 * shared_gauss(key, 23, (TOKENS, KV)) + 0.8 * shared_gauss(key, 4, (TOKENS, KV))
    strength = 0.1
    base_field = base_field - common_heads(key, 43, strength, head_direction(key))
    return (base_field * scales[None, :]).astype(jnp.bfloat16)


def padded_ids(key):
    first_key, second_key = jax.random.split(key)
    row_index = jnp.arange(TOKENS, dtype=jnp.int32)
    block_index = row_index // TOK_DP
    last_block = max(TOKENS // TOK_DP - 1, 1)
    threshold = 250 + 750 * block_index // last_block
    dice_roll = jax.random.randint(first_key, (TOKENS,), 0, 1000)
    kept_mask = (dice_roll < threshold) | (row_index % TOK_DP == 0)
    word_ids = jax.random.randint(second_key, (TOKENS,), 0, PAD_ID)
    return jnp.where(kept_mask, word_ids, PAD_ID).astype(jnp.int32)


def draw_current_ids(key, part):
    key = jax.random.fold_in(key, 5)
    return padded_ids(key)


def draw_replay_ids(key, part):
    key = jax.random.fold_in(key, 6)
    return padded_ids(key)


def block_scale(own_key, shape, cuts, least, high):
    def one(position, blocks):
        heights = jax.random.uniform(jax.random.fold_in(jax.random.fold_in(own_key, 6), position), (blocks,), jnp.float32, least / len(cuts), high / len(cuts))
        return jnp.repeat(jnp.exp(heights), shape[position] // blocks).reshape((-1,) + (1,) * (len(shape) - position - 1))

    factor_of = one(*cuts[0])
    for cut in cuts[1:]:
        factor_of = factor_of * one(*cut)
    return factor_of


def noise(own_key, dims, spread, limit, shards=(), kind=jnp.bfloat16):
    entries = spread * jax.random.normal(own_key, dims, jnp.float32)
    if shards:
        entries = entries * block_scale(own_key, dims, shards, -0.22, 0.18)
    return jnp.clip(entries, -limit, limit).astype(kind)


def setup_inputs(seed: int = 0) -> dict:
    streams_of = jax.random.split(jax.random.key(seed), 10)
    return {
        "current_acts": draw_current_acts(jax.random.fold_in(streams_of[9], 71), 0),
        "current_cot": draw_current_cot(jax.random.fold_in(streams_of[9], 71), 0),
        "current_ids": draw_current_ids(jax.random.fold_in(streams_of[9], 71), 0),
        "replay_acts": draw_replay_acts(jax.random.fold_in(streams_of[9], 71), 0),
        "replay_cot": draw_replay_cot(jax.random.fold_in(streams_of[9], 71), 0),
        "replay_ids": draw_replay_ids(jax.random.fold_in(streams_of[9], 71), 0),
        "master_weight": noise(streams_of[6], (D, KV), D ** -0.5, 0.09375, ((0, 64), (1, 8)), jnp.float32),
        "first_moment": noise(streams_of[7], (D, KV), 0.05, 0.75, ((0, 64), (1, 8)), jnp.float32),
        "second_moment": jnp.clip(jnp.exp(math.log(0.1) - 9.2103404 * jax.random.uniform(streams_of[8], (D, KV), jnp.float32) ** block_scale(streams_of[8], (D, KV), ((0, 64), (1, 8)), -0.2, 0.2)), 9.999999747378752e-06, 0.1),
    }


beta_first = 0.9
beta_second = 0.95
adam_eps = 1e-08
learn_rate = 0.001
decay_rate = 0.1
step_number = 10.0
norm_eps = 1e-12

def masked_grad(activations, cotangent, token_ids):
    kept_mask = (token_ids != PAD_ID).astype(jnp.bfloat16)
    masked = cotangent * kept_mask[:, None]
    return lax.dot_general(activations, masked, (((0,), (0,)), ((), ())), preferred_element_type=jnp.float32)

def reference(current_acts, current_cot, current_ids, replay_acts, replay_cot, replay_ids, master_weight, first_moment, second_moment):
    summed_current = masked_grad(current_acts, current_cot, current_ids)
    replay_grad = masked_grad(replay_acts, replay_cot, replay_ids)
    valid_count = jnp.sum((current_ids != PAD_ID).astype(jnp.float32))
    current_grad = summed_current / valid_count
    inner_sum = jnp.sum(current_grad * replay_grad)
    energy = jnp.sum(replay_grad * replay_grad)
    projected = current_grad - jnp.minimum(inner_sum, 0.0) / (energy + norm_eps) * replay_grad
    new_first = beta_first * first_moment + (1.0 - beta_first) * projected
    new_second = beta_second * second_moment + (1.0 - beta_second) * projected * projected
    fix_first = 1.0 - beta_first ** step_number
    fix_second = 1.0 - beta_second ** step_number
    update = new_first / fix_first / (jnp.sqrt(new_second / fix_second) + adam_eps)
    new_master = master_weight - learn_rate * (update + decay_rate * master_weight)
    return (new_master, new_first, new_second, new_master.astype(jnp.bfloat16))
```

```python
import jax
import jax.numpy as jnp
from jax import lax
from jax.experimental import pallas as pl
from jax.experimental.pallas import tpu as pltpu
from jax.sharding import PartitionSpec as P

PAD_ID = 128004
TOK = 768
FEAT = 512
HEAD = 128
ROWS = 64

beta_first = 0.9
beta_second = 0.95
adam_eps = 1e-08
learn_rate = 0.001
decay_rate = 0.1
step_number = 10.0
norm_eps = 1e-12

MESH = pl.DeviceIdType.MESH
HALF = TOK // 2

OWN, LOW, HIGH, FAR = range(4)
SHIFT = (0, 3, 1, 2)
ORDER = (
    (0, OWN),
    (1, OWN),
    (0, LOW),
    (0, HIGH),
    (0, FAR),
    (1, LOW),
    (1, HIGH),
    (1, FAR),
)


def kernel(
    cur_acts,
    cur_cot,
    cur_ids,
    rep_acts,
    rep_cot,
    rep_ids,
    master,
    first,
    second,
    new_master,
    new_first,
    new_second,
    gathered,
    acts,
    acts_t,
    cots,
    part_own,
    part_out,
    x_in,
    z_out,
    z_in,
    f_out,
    f_in,
    state,
    scal,
    load_sem,
    pair_send,
    pair_recv,
    y_send,
    y_recv,
    x_send,
    x_recv,
    z_send,
    z_recv,
    f_send,
    f_recv,
    s_send,
    s_recv,
    g_send,
    g_recv,
):
    dp = lax.axis_index("dp")
    tensor = lax.axis_index("tensor")
    z, yl, x = dp // 8, (dp // 4) % 2, dp % 4
    yh, c = tensor // 2, tensor % 2

    def device(z=z, yl=yl, x=x, yh=yh, c=c):
        return (z * 8 + yl * 4 + x, yh * 2 + c)

    def remote(src, dst, send, recv, target):
        return pltpu.make_async_remote_copy(
            src_ref=src,
            dst_ref=dst,
            send_sem=send,
            recv_sem=recv,
            device_id=target,
            device_id_type=MESH,
        )

    def z_peer(d):
        return device(z=(z + d) % 8)

    def x_peer(d):
        return device(x=(x + d) % 4)

    def xc_peer(d):
        return device(x=(x + d // 2) % 4, c=(c + d % 2) % 2)

    def y_peer(d):
        return device(yh=(yh + d // 2) % 4, yl=(yl + d % 2) % 2)

    act_refs, cot_refs, id_refs = (
        (cur_acts, rep_acts),
        (cur_cot, rep_cot),
        (cur_ids, rep_ids),
    )
    act_loads = [
        pltpu.make_async_copy(act_refs[b], acts.at[b], load_sem.at[b]) for b in range(2)
    ]
    cot_loads = [
        pltpu.make_async_copy(cot_refs[b], cots.at[b, OWN], load_sem.at[2 + b])
        for b in range(2)
    ]
    state_loads = [
        pltpu.make_async_copy(ref, state.at[i], load_sem.at[4 + i])
        for i, ref in enumerate((master, first, second))
    ]
    for copy in act_loads + cot_loads + state_loads:
        copy.start()

    goal_z, goal_yl = 2 * yh + z // 4, (z // 2) % 2
    goal_self = (goal_z == z) & (goal_yl == yl)

    barrier = pltpu.get_barrier_semaphore()
    for d in range(1, 8):
        for peer in (z_peer(d), xc_peer(d), y_peer(d)):
            pl.semaphore_signal(barrier, inc=1, device_id=peer, device_id_type=MESH)
    for q in range(2):
        for other in range(2):
            origin_z, origin_yh = (z % 2) * 4 + yl * 2 + q, z // 2
            origin_self = (origin_z == z) & (origin_yh == yh) & (yl == other)

            @pl.when(jnp.logical_not(origin_self))
            def _():
                pl.semaphore_signal(
                    barrier,
                    inc=1,
                    device_id=device(z=origin_z, yl=other, yh=origin_yh),
                    device_id_type=MESH,
                )

    @pl.when(goal_self)
    def _():
        pl.semaphore_wait(barrier, 24)

    @pl.when(jnp.logical_not(goal_self))
    def _():
        pl.semaphore_wait(barrier, 25)

    def half(h):
        return pl.ds(h * HALF, HALF)

    right, left = device(yh=(yh + 1) % 4), device(yh=(yh + 3) % 4)

    def to_right(b, h):
        return remote(
            cot_refs[b].at[half(h)],
            cots.at[b, LOW, half(h)],
            y_send.at[b, 0, h],
            y_recv.at[b, 0, h],
            right,
        )

    def to_left(b, h):
        return remote(
            cot_refs[b].at[half(h)],
            cots.at[b, HIGH, half(h)],
            y_send.at[b, 1, h],
            y_recv.at[b, 1, h],
            left,
        )

    def on_right(b):
        return remote(
            cots.at[b, LOW, half(0)],
            cots.at[b, FAR, half(0)],
            y_send.at[b, 2, 0],
            y_recv.at[b, 2, 0],
            right,
        )

    def on_left(b):
        return remote(
            cots.at[b, HIGH, half(1)],
            cots.at[b, FAR, half(1)],
            y_send.at[b, 2, 1],
            y_recv.at[b, 2, 1],
            left,
        )

    def send_own(b):
        to_right(b, 0).start()
        to_left(b, 1).start()
        to_right(b, 1).start()
        to_left(b, 0).start()

    def forward(b):
        to_right(b, 0).wait_recv()
        on_right(b).start()
        to_left(b, 1).wait_recv()
        on_left(b).start()

    send_own(0)

    def pair(b):
        return remote(
            acts_t.at[b, c],
            acts_t.at[b, c],
            pair_send.at[b],
            pair_recv.at[b],
            device(c=1 - c),
        )

    def pair_in(b):
        return remote(
            acts_t.at[b, 1 - c],
            acts_t.at[b, 1 - c],
            pair_send.at[b],
            pair_recv.at[b],
            device(c=1 - c),
        )

    def kept(b):
        return (id_refs[b][...] != PAD_ID).astype(jnp.float32)

    for b in range(2):
        act_loads[b].wait()
        mask = kept(b).astype(jnp.bfloat16)
        for j in range(4):
            block = acts[b, :, pl.ds(j * 128, 128)].T * mask
            for part in range(2):
                acts_t[b, c, 2 * (j % 2) + part, pl.ds((j // 2) * ROWS, ROWS), :] = (
                    block[part * ROWS : (part + 1) * ROWS]
                )
        pair(b).start()

    def x_copy(b, rel, d):
        return remote(
            part_out.at[b, rel, d],
            x_in.at[b, rel, d],
            x_send.at[b, rel, d],
            x_recv.at[b, rel, d],
            x_peer(d),
        )

    def multiply(b, rel):
        cot = cots[b, rel]
        for d in (2, 1, 3, 0):
            block = (x + d) % 4
            for group in range(2):
                tile = jnp.dot(
                    acts_t[b, group, block], cot, preferred_element_type=jnp.float32
                )
                rows = pl.ds(group * 128, 128)
                if d:
                    part_out[b, rel, d, rows] = tile.astype(jnp.bfloat16)
                else:
                    part_own[b, rel, rows] = tile
            if d:
                x_copy(b, rel, d).start()

    def z_copy(b, rel, d):
        return remote(
            z_out.at[b, rel, (z + d) % 8],
            z_in.at[b, rel, d],
            z_send.at[b, rel, d],
            z_recv.at[b, rel, d],
            z_peer(d),
        )

    def add_x(b, rel):
        for d in range(1, 4):
            x_copy(b, rel, d).wait_recv()
        total = part_own[b, rel]
        for d in range(1, 4):
            total = total + x_in[b, rel, d].astype(jnp.float32)
        z_out[b, rel] = total.reshape(8, 32, 128)
        for d in (4, 3, 5, 2, 6, 1, 7):
            z_copy(b, rel, d).start()

    def goal(rel):
        return device(z=goal_z, yl=goal_yl, yh=(yh + SHIFT[rel]) % 4)

    def f_copy(b, rel):
        return remote(
            f_out.at[b, rel],
            f_in.at[b, yl, z % 2],
            f_send.at[b, rel],
            f_recv.at[b, yl, z % 2],
            goal(rel),
        )

    def f_local(b):
        return pltpu.make_async_copy(
            f_out.at[b, OWN], f_in.at[b, yl, z % 2], f_recv.at[b, yl, z % 2]
        )

    def add_z(b, rel):
        for d in range(1, 8):
            z_copy(b, rel, d).wait_recv()
        total = z_out[b, rel, z]
        for d in range(1, 8):
            total = total + z_in[b, rel, d]
        f_out[b, rel] = total
        if rel == OWN:

            @pl.when(goal_self)
            def _():
                f_local(b).start()

            @pl.when(jnp.logical_not(goal_self))
            def _():
                f_copy(b, rel).start()

        else:
            f_copy(b, rel).start()

    def arrive(b, rel):
        if rel == OWN:
            cot_loads[b].wait()
            pair_in(b).wait_recv()
        elif rel == LOW:
            if b == 0:
                forward(0)
                send_own(1)
            else:
                forward(1)
            to_right(b, 1).wait_recv()
        elif rel == HIGH:
            to_left(b, 0).wait_recv()
        else:
            on_right(b).wait_recv()
            on_left(b).wait_recv()

    count = len(ORDER)
    for step in range(count + 2):
        if step < count:
            arrive(*ORDER[step])
            multiply(*ORDER[step])
        if 1 <= step < count + 1:
            add_x(*ORDER[step - 1])
        if step >= 2:
            add_z(*ORDER[step - 2])

    sums = []
    for b in range(2):
        for other in range(2):
            for q in range(2):
                pltpu.make_async_copy(
                    f_in.at[b, other, q], f_in.at[b, other, q], f_recv.at[b, other, q]
                ).wait()
        sums.append((f_in[b, 0] + f_in[b, 1]).reshape(ROWS, HEAD))
    summed, replay = sums

    mask = kept(0)
    lanes = mask[:, 0:128]
    for j in range(1, 6):
        lanes = lanes + mask[:, j * 128 : (j + 1) * 128]
    scal[0, 0] = jnp.concatenate(
        [
            jnp.sum(summed * replay, axis=0, keepdims=True),
            jnp.sum(replay * replay, axis=0, keepdims=True),
            lanes,
            jnp.zeros((5, 128), jnp.float32),
        ],
        axis=0,
    )

    def s_copy(k, d):
        return remote(
            scal.at[k, 0],
            scal.at[k, d],
            s_send.at[k, d],
            s_recv.at[k, d],
            (z_peer, xc_peer, y_peer)[k](d),
        )

    for k in range(3):
        for d in range(7, 0, -1):
            s_copy(k, d).start()
        for d in range(1, 8):
            s_copy(k, d).wait_recv()
        total = scal[k, 0]
        for d in range(1, 8):
            total = total + scal[k, d]
        scal[k + 1, 0] = total
    totals = jnp.sum(total, axis=1, keepdims=True)
    valid_count = totals[2:3] * 0.125
    inner_sum = totals[0:1] / valid_count
    energy = totals[1:2]
    factor = jnp.minimum(inner_sum, 0.0) / (energy + norm_eps)

    for copy in state_loads:
        copy.wait()
    projected = summed / valid_count - factor * replay
    moment = beta_first * state[1] + (1.0 - beta_first) * projected
    spread = beta_second * state[2] + (1.0 - beta_second) * projected * projected
    fix_first = 1.0 - beta_first**step_number
    fix_second = 1.0 - beta_second**step_number
    update = moment / fix_first / (jnp.sqrt(spread / fix_second) + adam_eps)
    weight = state[0] - learn_rate * (update + decay_rate * state[0])
    gathered[z, yl, x] = weight.astype(jnp.bfloat16)

    def gz_copy(d):
        return remote(
            gathered.at[z, yl, x],
            gathered.at[z, yl, x],
            g_send.at[d],
            g_recv.at[d],
            z_peer(d),
        )

    def gz_in(d):
        block = gathered.at[(z + 8 - d) % 8, yl, x]
        return remote(block, block, g_send.at[d], g_recv.at[d], z_peer(d))

    def gy_copy(src_yl):
        block = gathered.at[:, src_yl, x]
        return remote(block, block, g_send.at[0], g_recv.at[0], device(yl=1 - yl))

    def gx_copy(k, src_yl, src_x, d):
        block = gathered.at[:, src_yl, src_x]
        i = 8 + 4 * k + d
        return remote(block, block, g_send.at[i], g_recv.at[i], x_peer(d))

    for d in (4, 3, 5, 2, 6, 1, 7):
        gz_copy(d).start()
    new_master[...] = weight
    new_first[...] = moment
    new_second[...] = spread
    for d in range(1, 8):
        gz_in(d).wait_recv()
    gy_copy(yl).start()
    for d in (2, 1, 3):
        gx_copy(0, yl, x, d).start()
    gy_copy(1 - yl).wait_recv()
    for d in (2, 1, 3):
        gx_copy(1, 1 - yl, x, d).start()
    for d in range(1, 4):
        gx_copy(0, yl, (x + 4 - d) % 4, d).wait_recv()
        gx_copy(1, 1 - yl, (x + 4 - d) % 4, d).wait_recv()

    for b in range(2):
        pair(b).wait_send()
        for h in range(2):
            to_right(b, h).wait_send()
            to_left(b, h).wait_send()
        on_right(b).wait_send()
        on_left(b).wait_send()
        for rel in range(4):
            for d in range(1, 4):
                x_copy(b, rel, d).wait_send()
            for d in range(1, 8):
                z_copy(b, rel, d).wait_send()
            if rel == OWN:

                @pl.when(jnp.logical_not(goal_self))
                def _():
                    f_copy(b, rel).wait_send()

            else:
                f_copy(b, rel).wait_send()
    for d in range(1, 8):
        for k in range(3):
            s_copy(k, d).wait_send()
        gz_copy(d).wait_send()
    gy_copy(yl).wait_send()
    for d in range(1, 4):
        gx_copy(0, yl, x, d).wait_send()
        gx_copy(1, 1 - yl, x, d).wait_send()


def on_device(
    current_acts,
    current_cot,
    current_ids,
    replay_acts,
    replay_cot,
    replay_ids,
    master_weight,
    first_moment,
    second_moment,
):
    hbm = pl.BlockSpec(memory_space=pl.ANY)
    vmem = pl.BlockSpec(memory_space=pltpu.VMEM)
    rows = jax.ShapeDtypeStruct((ROWS, HEAD), jnp.float32)
    dma = pltpu.SemaphoreType.DMA
    new_master, new_first, new_second, gathered = pl.pallas_call(
        kernel,
        out_shape=(
            rows,
            rows,
            rows,
            jax.ShapeDtypeStruct((8, 2, 4, ROWS, HEAD), jnp.bfloat16),
        ),
        in_specs=[hbm, hbm, vmem, hbm, hbm, vmem, hbm, hbm, hbm],
        out_specs=(vmem, vmem, vmem, vmem),
        scratch_shapes=[
            pltpu.VMEM((2, TOK, FEAT), jnp.bfloat16),
            pltpu.VMEM((2, 2, 4, 2 * ROWS, TOK), jnp.bfloat16),
            pltpu.VMEM((2, 4, TOK, HEAD), jnp.bfloat16),
            pltpu.VMEM((2, 4, 256, HEAD), jnp.float32),
            pltpu.VMEM((2, 4, 4, 256, HEAD), jnp.bfloat16),
            pltpu.VMEM((2, 4, 4, 256, HEAD), jnp.bfloat16),
            pltpu.VMEM((2, 4, 8, 32, HEAD), jnp.float32),
            pltpu.VMEM((2, 4, 8, 32, HEAD), jnp.float32),
            pltpu.VMEM((2, 4, 32, HEAD), jnp.float32),
            pltpu.VMEM((2, 2, 2, 32, HEAD), jnp.float32),
            pltpu.VMEM((3, ROWS, HEAD), jnp.float32),
            pltpu.VMEM((4, 8, 8, HEAD), jnp.float32),
            dma((7,)),
            dma((2,)),
            dma((2,)),
            dma((2, 3, 2)),
            dma((2, 3, 2)),
            dma((2, 4, 4)),
            dma((2, 4, 4)),
            dma((2, 4, 8)),
            dma((2, 4, 8)),
            dma((2, 4)),
            dma((2, 2, 2)),
            dma((3, 8)),
            dma((3, 8)),
            dma((16,)),
            dma((16,)),
        ],
        compiler_params=pltpu.CompilerParams(
            collective_id=0,
            has_side_effects=True,
            vmem_limit_bytes=40 * 1024 * 1024,
        ),
    )(
        current_acts,
        current_cot,
        current_ids.reshape(1, TOK),
        replay_acts,
        replay_cot,
        replay_ids.reshape(1, TOK),
        master_weight,
        first_moment,
        second_moment,
    )
    return (new_master, new_first, new_second, gathered.reshape(64 * ROWS, HEAD))


def solution(mesh):
    placed = (
        P("dp", "tensor"),
        P("dp", "tensor"),
        P("dp"),
        P("dp", "tensor"),
        P("dp", "tensor"),
        P("dp"),
        P("dp", "tensor"),
        P("dp", "tensor"),
        P("dp", "tensor"),
    )
    return jax.shard_map(
        on_device,
        mesh=mesh,
        in_specs=placed,
        out_specs=(P("dp", "tensor"), P("dp", "tensor"), P("dp", "tensor"), P(None, "tensor")),
        check_vma=False,
    )
```
